256 devices in a mesh: row: 16 (over z, x_hi), col: 8 (over y, x_lo), depth: 2 (over core).
Axes of the slice: x: 4 (x_hi: 2, x_lo: 2; x = x_hi * 2 + x_lo), y: 4, z: 8, core: 2. Of those that a mesh axis runs over, the one named last changes fastest.
Arguments:
- amplitudes: float32 [512, 65536], P('row', ('col', 'depth')), may hold values from -6 to 6
- integrals: float32 [12288, 65536], P('row', ('col', 'depth')), may hold values from -0.0234375 to 0.0234375
- pair_energy: float32 [512], P(('col', 'depth')), may hold values from -4 to -1
- virt_energy: float32 [12288], P('row'), may hold values from 0.4 to 6
Outputs:
- residual: float32 [512, 12288], P(('col', 'depth'), 'row')
The draws below stay inside these ranges and needn't reach their ends.
All inputs are finite; a program needn't handle non-finite values.
Results may differ from the reference program's by a relative error of at most 0.00011.
Values sent between devices are 32-bit elements; how exact they have to be, the bound alone decides.
No kernel may reach another device: no remote copies, remote signals or barrier semaphores. Data moves between devices by JAX's collectives and lax.ppermute only.
A program may use at most 128 MiB of HBM per device.

```python
import jax
import jax.numpy as jnp
from jax import lax

CD = 65536
AB = 12288
PAIRS = 512


def strengthened(drawn, stream_key, source, target, parts, factor):
    def block_of(position):
        return (jnp.arange(drawn.shape[position]) // (drawn.shape[position] // parts)).reshape((-1,) + (1,) * (drawn.ndim - 1 - position))

    first = jax.random.permutation(stream_key, parts)[block_of(target)]
    second = (block_of(target) + parts // 2) % parts
    return jnp.where((block_of(source) == first) | (block_of(source) == second), factor * drawn, drawn)


def levels(stream_key, extent, split, low, largest):
    def one(dim, shards_of):
        heights = jax.random.uniform(jax.random.fold_in(jax.random.fold_in(stream_key, 6), dim), (shards_of,), jnp.float32, low / len(split), largest / len(split))
        return jnp.repeat(jnp.exp(heights), extent[dim] // shards_of).reshape((-1,) + (1,) * (len(extent) - dim - 1))

    level = one(*split[0])
    for cut in split[1:]:
        level = level * one(*cut)
    return level


def scatter_about(own_key, shape, spread, reach, shards=(), dtype=jnp.bfloat16):
    array = spread * jax.random.normal(own_key, shape, jnp.float32)
    if shards:
        array = array * levels(own_key, shape, shards, -0.22, 0.18)
    return jnp.clip(array, -reach, reach).astype(dtype)


def noise_with(key, dims, scale, reach, shards, heavy, kind=jnp.bfloat16):
    result = scale * jax.random.normal(key, dims, jnp.float32)
    if shards:
        result = result * levels(key, dims, shards, -0.22, 0.18)
    return jnp.clip(strengthened(result, jax.random.fold_in(key, 3), *heavy), -reach, reach).astype(kind)


def setup_inputs(seed: int = 0) -> dict:
    splits = jax.random.split(jax.random.key(seed), 5)
    amplitudes = noise_with(splits[0], (PAIRS, CD), 1.0, 6.0, ((0, 16), (1, 16)), (1, 0, 16, 2.0), jnp.float32)
    integrals = scatter_about(splits[1], (AB, CD), CD ** -0.5, 0.0234375, ((0, 16), (1, 16)), jnp.float32)
    pair_energy = jnp.clip(-4.0 + 3.0 * jax.random.uniform(splits[2], (PAIRS,), jnp.float32) ** levels(splits[2], (PAIRS,), ((0, 16),), -0.2, 0.2), -4.0, -1.0)
    virt_energy = jnp.clip(0.4 + 5.6 * jax.random.uniform(splits[3], (AB,), jnp.float32) ** levels(splits[3], (AB,), ((0, 16),), -0.2, 0.2), 0.4, 6.0)
    return dict(amplitudes=amplitudes, integrals=integrals, pair_energy=pair_energy, virt_energy=virt_energy)


def reference(amplitudes, integrals, pair_energy, virt_energy):
    ladder = lax.dot_general(amplitudes, integrals, (((1,), (1,)), ((), ())), precision=lax.Precision.HIGHEST, preferred_element_type=jnp.float32)
    denominators = pair_energy[:, None] - virt_energy[None, :]
    return ladder / denominators
```

```python
import jax
import jax.numpy as jnp
from jax import lax
from jax.sharding import PartitionSpec as P

NZ, NXH, NY, NXL = 8, 2, 4, 2


def z_shift(block, step):
    perm = [(z * NXH + h, ((z + step) % NZ) * NXH + h) for z in range(NZ) for h in range(NXH)]
    return lax.ppermute(block, "row", perm)


def x_peer(block):
    perm = [(z * NXH + h, z * NXH + 1 - h) for z in range(NZ) for h in range(NXH)]
    return lax.ppermute(block, "row", perm)


def y_shift(block, step):
    perm = [(y * NXL + x, ((y + step) % NY) * NXL + x) for y in range(NY) for x in range(NXL)]
    return lax.ppermute(block, "col", perm)


def x_near(block):
    perm = [(y * NXL + x, y * NXL + 1 - x) for y in range(NY) for x in range(NXL)]
    return lax.ppermute(block, "col", perm)


def core_peer(block):
    return lax.ppermute(block, "depth", [(0, 1), (1, 0)])


def split(values):
    high = lax.reduce_precision(values, 8, 7)
    return high.astype(jnp.bfloat16), (values - high).astype(jnp.bfloat16)


def product(left, right):
    return lax.dot_general(left, right, (((1,), (1,)), ((), ())), preferred_element_type=jnp.float32)


def local(amplitudes, integrals, pair_energy, virt_energy):
    rows, width = amplitudes.shape
    columns = integrals.shape[0]
    half = rows // 2
    quarter = half // 2
    row, col, depth = (lax.axis_index(name) for name in ("row", "col", "depth"))
    z, h = row // NXH, row % NXH
    y, x = col // NXL, col % NXL
    right_high, right_low = split(integrals)

    def early(block):
        return block[:half]

    def late(block):
        return block[half:]

    own = {0: amplitudes}
    peer_early = {0: x_peer(early(amplitudes))}
    peer_late = {0: x_peer(late(amplitudes))}
    for d in (1, 2, 3):
        for s in (1, -1):
            own[s * d] = z_shift(own[s * (d - 1)], -s)
            peer_early[s * d] = z_shift(peer_early[s * (d - 1)], -s)
            peer_late[s * d] = x_peer(late(own[s * d]))
    far_early = z_shift(early(own[3]), -1)
    far_late = z_shift(late(own[-3]), 1)
    own[4] = jnp.concatenate([far_early, far_late])
    peer_late[4] = x_peer(far_late)
    peer_early[4] = jnp.concatenate(
        [z_shift(peer_early[3][:quarter], -1), z_shift(peer_early[-3][quarter:], 1)]
    )

    def ladder(blocks):
        left_high, left_low = split(jnp.concatenate(blocks))
        count = left_high.shape[0]
        both = product(jnp.concatenate([left_high, left_low]), right_high)
        return both[:count] + both[count:] + product(left_high, right_low)

    groups = (
        (("o", 0), ("o", 1), ("o", -1), ("e", 0), ("l", 0)),
        (("o", 2), ("o", -2), ("e", 1), ("e", -1), ("l", 1), ("l", -1)),
        (("o", 3), ("o", -3), ("e", 2), ("e", -2), ("l", 2), ("l", -2)),
        (("o", 4), ("e", 3), ("e", -3), ("e", 4), ("l", 3), ("l", -3), ("l", 4)),
    )
    held = {"o": own, "e": peer_early, "l": peer_late}
    partial = jnp.zeros((2, NZ, rows, columns), jnp.float32)
    for group in groups:
        sums = ladder([held[kind][d] for kind, d in group])
        at = 0
        for kind, d in group:
            count = rows if kind == "o" else half
            place = ((0 if kind == "o" else 1), (z + d) % NZ, half if kind == "l" else 0, 0)
            partial = lax.dynamic_update_slice(partial, sums[at : at + count][None, None], place)
            at += count

    mine = h ^ depth
    kept = lax.dynamic_index_in_dim(partial, mine, 0, keepdims=False)
    given = lax.dynamic_index_in_dim(partial, 1 - mine, 0, keepdims=False)
    total = (kept + core_peer(given)).reshape(NY, NXL, rows, columns)

    def to_y(step):
        return lax.dynamic_index_in_dim(total, (y + step) % NY, 0, keepdims=False)

    total = to_y(0) + y_shift(to_y(1), 1) + y_shift(to_y(-1), -1) + y_shift(to_y(2), 2)
    given = lax.dynamic_index_in_dim(total, 1 - x, 0, keepdims=False)
    total = lax.dynamic_index_in_dim(total, x, 0, keepdims=False) + x_near(given)
    return total / (pair_energy[:, None] - virt_energy[None, :])


def solution(mesh):
    in_specs = (
        P("row", ("col", "depth")),
        P("row", ("col", "depth")),
        P(("col", "depth")),
        P("row"),
    )
    out_specs = P(("col", "depth"), "row")
    return jax.shard_map(local, mesh=mesh, in_specs=in_specs, out_specs=out_specs, check_vma=False)
```

```python
import functools

import jax
import jax.numpy as jnp
from jax import lax
from jax.experimental import pallas as pl
from jax.experimental.pallas import tpu as pltpu
from jax.sharding import PartitionSpec as P

NZ, NXH, NY, NXL = 8, 2, 4, 2
MIB = 1 << 20
VMEM = pl.BlockSpec(memory_space=pltpu.VMEM)
SMEM = pl.BlockSpec(memory_space=pltpu.SMEM)
HBM = pl.BlockSpec(memory_space=pltpu.HBM)
ANY = pl.BlockSpec(memory_space=pl.ANY)


def z_shift(block, step):
    perm = [(z * NXH + h, ((z + step) % NZ) * NXH + h) for z in range(NZ) for h in range(NXH)]
    return lax.ppermute(block, "row", perm)


def x_peer(block):
    perm = [(z * NXH + h, z * NXH + 1 - h) for z in range(NZ) for h in range(NXH)]
    return lax.ppermute(block, "row", perm)


def y_shift(block, step):
    perm = [(y * NXL + x, ((y + step) % NY) * NXL + x) for y in range(NY) for x in range(NXL)]
    return lax.ppermute(block, "col", perm)


def x_near(block):
    perm = [(y * NXL + x, y * NXL + 1 - x) for y in range(NY) for x in range(NXL)]
    return lax.ppermute(block, "col", perm)


def core_peer(block):
    return lax.ppermute(block, "depth", [(0, 1), (1, 0)])


def halves(values):
    high = values.astype(jnp.bfloat16)
    return high, (values - high.astype(jnp.float32)).astype(jnp.bfloat16)


def dot(a, b):
    return lax.dot_general(a, b, (((1,), (1,)), ((), ())), preferred_element_type=jnp.float32)


def group_kernel(plan, place, *refs, held):
    names = sorted({name for pieces in plan for name, *_ in pieces[2]})
    blocks = dict(zip(names, refs))
    high, low = refs[len(names) : len(names) + 2]
    out, token, left = refs[-3:]
    token[...] = jnp.zeros_like(token)
    total = left.shape[0] // 2
    at = 0
    for kind, d, pieces, start in plan:
        values = [blocks[name][first : first + count] for name, first, count in pieces]
        values = values[0] if len(values) == 1 else jnp.concatenate(values)
        count = values.shape[0]
        left[at : at + count], left[total + at : total + at + count] = halves(values)
        at += count
    z, flip = place[0], place[1]

    def tile(n, _):
        spot = pl.ds(pl.multiple_of(n * 256, 256), 256)
        both = dot(left[...], high[spot])
        sums = both[:total] + both[total:] + dot(left[:total], low[spot])
        at = 0
        for kind, d, pieces, start in plan:
            count = sum(p[2] for p in pieces)
            out[kind ^ flip, lax.rem(z + d + NZ, NZ), start : start + count, spot] = sums[at : at + count]
            at += count
        return 0

    lax.fori_loop(0, high.shape[0] // 256, tile, 0)


def group(plan, place, blocks, weights, partial, rows):
    names = sorted({name for pieces in plan for name, *_ in pieces[2]})
    columns, width = weights[0].shape
    total = sum(p[2] for _, _, pieces, _ in plan for p in pieces)
    operands = [place] + [blocks[name] for name in names] + list(weights)
    in_specs = [SMEM] + [VMEM] * (len(names) + 2)
    aliases = {}
    if partial is not None:
        aliases = {len(operands): 0}
        operands.append(partial)
        in_specs.append(VMEM)
    return pl.pallas_call(
        functools.partial(group_kernel, plan, held=partial is not None),
        out_shape=[
            jax.ShapeDtypeStruct((2, NZ, rows, columns), jnp.float32),
            jax.ShapeDtypeStruct((8, 128), jnp.float32),
        ],
        in_specs=in_specs,
        out_specs=[VMEM, VMEM],
        scratch_shapes=[pltpu.VMEM((2 * total, width), jnp.bfloat16)],
        input_output_aliases=aliases,
        compiler_params=pltpu.CompilerParams(vmem_limit_bytes=10 * MIB),
        cost_estimate=pl.CostEstimate(flops=4 * 3 * total * columns * width, bytes_accessed=MIB, transcendentals=0),
    )(*operands)


def first_kernel(plan, place, a0, up, down, peer, source, out, token, high, low, left, held, sems):
    steps, slots = 8, held.shape[0]
    count = source.shape[1] // steps

    def copy(step):
        slot = step % slots
        return pltpu.make_async_copy(source.at[:, pl.ds(step * count, count)], held.at[slot], sems.at[slot])

    for step in range(slots - 1):
        copy(step).start()
    token[...] = jnp.zeros_like(token)
    rows = a0.shape[0]
    total = 4 * rows
    for i, block in enumerate((a0, up, down, peer)):
        spot = pl.ds(i * rows, rows)
        left[spot], left[pl.ds(total + i * rows, rows)] = halves(block[...])
    z, flip = place[0], place[1]
    for step in range(steps):
        if step + slots - 1 < steps:
            copy(step + slots - 1).start()
        copy(step).wait()
        spot = pl.ds(step * count, count)
        high[:, spot], low[:, spot] = halves(held[step % slots])
        both = dot(left[:, spot], high[:, spot])
        sums = both[:total] + both[total:] + dot(left[:total, spot], low[:, spot])
        for i, (kind, d) in enumerate(plan):
            at = (kind ^ flip, lax.rem(z + d + NZ, NZ))
            part = sums[i * rows : (i + 1) * rows]
            out[at] = part if step == 0 else out[at] + part


def first_group(plan, place, blocks, integrals):
    rows, width = blocks[0].shape
    columns = integrals.shape[0]
    return pl.pallas_call(
        functools.partial(first_kernel, plan),
        out_shape=[
            jax.ShapeDtypeStruct((2, NZ, rows, columns), jnp.float32),
            jax.ShapeDtypeStruct((8, 128), jnp.float32),
            jax.ShapeDtypeStruct(integrals.shape, jnp.bfloat16),
            jax.ShapeDtypeStruct(integrals.shape, jnp.bfloat16),
        ],
        in_specs=[SMEM] + [VMEM] * 4 + [HBM],
        out_specs=[VMEM] * 4,
        scratch_shapes=[
            pltpu.VMEM((8 * rows, width), jnp.bfloat16),
            pltpu.VMEM((4, columns, width // 8), jnp.float32),
            pltpu.SemaphoreType.DMA((4,)),
        ],
        compiler_params=pltpu.CompilerParams(vmem_limit_bytes=40 * MIB),
        cost_estimate=pl.CostEstimate(flops=48 * rows * columns * width, bytes_accessed=12 * MIB, transcendentals=0),
    )(place, *blocks, integrals)


def stage_kernel(kept, cuts, *refs):
    inputs, outputs = refs[: len(refs) - kept - len(cuts)], refs[len(refs) - len(cuts) :]
    for out, parts in zip(outputs, cuts):
        at = 0
        for source, first, count in parts:
            out[at : at + count] = inputs[source][first : first + count]
            at += count


def stage(kept, others, cuts, weights, tokens):
    width = kept[0].shape[1]
    return pl.pallas_call(
        functools.partial(stage_kernel, len(kept), cuts),
        out_shape=[jax.ShapeDtypeStruct(v.shape, v.dtype) for v in kept]
        + [jax.ShapeDtypeStruct((sum(p[2] for p in parts), width), jnp.float32) for parts in cuts],
        in_specs=[VMEM] * (len(kept) + len(others) + len(weights)) + [ANY] * len(tokens),
        out_specs=[VMEM] * (len(kept) + len(cuts)),
        input_output_aliases={i: i for i in range(len(kept))},
        compiler_params=pltpu.CompilerParams(vmem_limit_bytes=4 * MIB),
        cost_estimate=pl.CostEstimate(flops=0, bytes_accessed=MIB, transcendentals=0),
    )(*kept, *others, *weights, *tokens)


def local(amplitudes, integrals, pair_energy, virt_energy):
    rows, width = amplitudes.shape
    columns = integrals.shape[0]
    half = rows // 2
    quarter = half // 2
    row, col, depth = (lax.axis_index(name) for name in ("row", "col", "depth"))
    z, h = row // NXH, row % NXH
    y, x = col // NXL, col % NXL
    place = jnp.stack([z, h ^ depth]).astype(jnp.int32)

    def ring(up, down):
        return z_shift(up, -1), z_shift(down, 1)

    def whole(kind, d, name):
        return (kind, d, ((name, 0, rows),), 0)

    def early(d, name):
        return (1, d, ((name, 0, half),), 0)

    def lates(d, name):
        return [(1, d, ((name, 0, half),), half), (1, -d, ((name, half, half),), half)]

    late = ((0, half, half), (1, half, half))
    a1 = ring(amplitudes, amplitudes)
    x0 = x_peer(amplitudes)
    *a1, b0, late1 = stage(a1, [x0], (((2, 0, half),), late), [], [])
    a2 = ring(*a1)
    b1 = ring(b0, b0)
    x1 = x_peer(late1)
    partial, token, *weights = first_group(
        ((0, 0), (0, 1), (0, -1), (1, 0)), place, [amplitudes, *a1, x0], integrals)
    b1 = stage(b1, [], (), weights, [token])
    b2 = ring(*b1)
    *a2, late2 = stage(a2, [], (late,), weights, b1)
    a3 = ring(*a2)
    x2 = x_peer(late2)
    partial, token = group(
        [whole(0, 2, "u"), whole(0, -2, "d"), *lates(1, "x"), early(1, "bu"), early(-1, "bd")],
        place, dict(u=a2[0], d=a2[1], x=x1, bu=b1[0], bd=b1[1]), weights, partial, rows)
    b2 = stage(b2, [], (), weights, [token])
    b3 = ring(*b2)
    *a3, up, down, late3 = stage(a3, [], (((0, 0, half),), ((1, half, half),), late), weights, b2)
    a4 = z_shift(up, -1), z_shift(down, 1)
    x3 = x_peer(late3)
    partial, token = group(
        [whole(0, 3, "u"), whole(0, -3, "d"), *lates(2, "x"), early(2, "bu"), early(-2, "bd")],
        place, dict(u=a3[0], d=a3[1], x=x2, bu=b2[0], bd=b2[1]), weights, partial, rows)
    *b3, up, down = stage(b3, [], (((0, 0, quarter),), ((1, quarter, quarter),)), weights, [token])
    b4 = z_shift(up, -1), z_shift(down, 1)
    x4 = x_peer(a4[1])
    partial, token = group(
        [
            (0, 4, (("a4u", 0, half), ("a4d", 0, half)), 0),
            early(3, "bu"),
            early(-3, "bd"),
            *lates(3, "x3"),
            (1, 4, (("b4u", 0, quarter), ("b4d", 0, quarter), ("x4", 0, half)), 0),
        ],
        place, dict(a4u=a4[0], a4d=a4[1], bu=b3[0], bd=b3[1], x3=x3, b4u=b4[0], b4d=b4[1], x4=x4), weights, partial, rows)

    total = (partial[0] + core_peer(partial[1])).reshape(NY, NXL, rows, columns)

    def at_y(value, step):
        return lax.dynamic_index_in_dim(value, (y + step) % NY, 0, keepdims=False)

    total = at_y(total, 0) + (y_shift(at_y(total, 2), 2) + y_shift(at_y(total, 1), 1) + y_shift(at_y(total, -1), -1))
    given = lax.dynamic_index_in_dim(total, 1 - x, 0, keepdims=False)
    total = lax.dynamic_index_in_dim(total, x, 0, keepdims=False) + x_near(given)
    return total / (pair_energy[:, None] - virt_energy[None, :])


def solution(mesh):
    in_specs = (
        P("row", ("col", "depth")),
        P("row", ("col", "depth")),
        P(("col", "depth")),
        P("row"),
    )
    out_specs = P(("col", "depth"), "row")
    return jax.shard_map(local, mesh=mesh, in_specs=in_specs, out_specs=out_specs, check_vma=False)
```

```python
import functools

import jax
import jax.numpy as jnp
from jax import lax
from jax.experimental import pallas as pl
from jax.experimental.pallas import tpu as pltpu
from jax.sharding import PartitionSpec as P

NZ, NXH, NY, NXL = 8, 2, 4, 2
MIB = 1 << 20
VMEM = pl.BlockSpec(memory_space=pltpu.VMEM)
SMEM = pl.BlockSpec(memory_space=pltpu.SMEM)
HBM = pl.BlockSpec(memory_space=pltpu.HBM)
ANY = pl.BlockSpec(memory_space=pl.ANY)


def z_shift(block, step):
    perm = [(z * NXH + h, ((z + step) % NZ) * NXH + h) for z in range(NZ) for h in range(NXH)]
    return lax.ppermute(block, "row", perm)


def x_peer(block):
    perm = [(z * NXH + h, z * NXH + 1 - h) for z in range(NZ) for h in range(NXH)]
    return lax.ppermute(block, "row", perm)


def col_shift(block, dy, dx):
    perm = [(y * NXL + x, ((y + dy) % NY) * NXL + (x ^ dx)) for y in range(NY) for x in range(NXL)]
    return lax.ppermute(block, "col", perm)


def core_peer(block):
    return lax.ppermute(block, "depth", [(0, 1), (1, 0)])


def halves(values):
    high = values.astype(jnp.bfloat16)
    return high, (values - high.astype(jnp.float32)).astype(jnp.bfloat16)


def dot(a, b):
    return lax.dot_general(a, b, (((1,), (1,)), ((), ())), preferred_element_type=jnp.float32)


def names_of(plan):
    return sorted({name for _, _, pieces, _ in plan for both, *_ in pieces for name in both.split()})


def group_kernel(plan, place, *refs, held, first, adding):
    names = names_of(plan)
    blocks = dict(zip(names, refs))
    high, low = refs[len(names) : len(names) + 2]
    out, token, left = refs[-3:]
    span = pl.ds(first, left.shape[1])
    token[...] = jnp.zeros_like(token)
    total = left.shape[0] // 2
    at = 0
    for kind, d, pieces, start in plan:
        values = [
            jnp.concatenate([blocks[name][low_row : low_row + count] for name in both.split()], axis=1)
            for both, low_row, count in pieces
        ]
        values = values[0] if len(values) == 1 else jnp.concatenate(values)
        count = values.shape[0]
        left[at : at + count], left[total + at : total + at + count] = halves(values)
        at += count
    z, flip = place[0], place[1]

    def tile(n, _):
        spot = pl.ds(pl.multiple_of(n * 768, 768), 768)
        both = dot(left[...], high[spot, span])
        sums = both[:total] + both[total:] + dot(left[:total], low[spot, span])
        at = 0
        for kind, d, pieces, start in plan:
            count = sum(p[2] for p in pieces)
            where = (kind ^ flip, lax.rem(z + d + NZ, NZ), slice(start, start + count), spot)
            out[where] = sums[at : at + count] + out[where] if adding else sums[at : at + count]
            at += count
        return 0

    lax.fori_loop(0, high.shape[0] // 768, tile, 0)


def group(plan, place, blocks, weights, partial, rows, first=0, adding=False):
    names = names_of(plan)
    columns = weights[0].shape[0]
    width = max(block.shape[1] for block in blocks.values())
    total = sum(p[2] for _, _, pieces, _ in plan for p in pieces)
    operands = [place] + [blocks[name] for name in names] + list(weights)
    in_specs = [SMEM] + [VMEM] * (len(names) + 2)
    aliases = {}
    if partial is not None:
        aliases = {len(operands): 0}
        operands.append(partial)
        in_specs.append(VMEM)
    return pl.pallas_call(
        functools.partial(group_kernel, plan, held=partial is not None, first=first, adding=adding),
        out_shape=[
            jax.ShapeDtypeStruct((2, NZ, rows, columns), jnp.float32),
            jax.ShapeDtypeStruct((8, 128), jnp.float32),
        ],
        in_specs=in_specs,
        out_specs=[VMEM, VMEM],
        scratch_shapes=[pltpu.VMEM((2 * total, width), jnp.bfloat16)],
        input_output_aliases=aliases,
        compiler_params=pltpu.CompilerParams(vmem_limit_bytes=10 * MIB),
        cost_estimate=pl.CostEstimate(flops=4 * 3 * total * columns * width, bytes_accessed=MIB, transcendentals=0),
    )(*operands)


def first_kernel(plan, place, a0, source, out, token, high, low, left, held, sems):
    steps, slots = 8, held.shape[0]
    count = source.shape[1] // steps

    def copy(step):
        slot = step % slots
        return pltpu.make_async_copy(source.at[:, pl.ds(step * count, count)], held.at[slot], sems.at[slot])

    for step in range(slots - 1):
        copy(step).start()
    token[...] = jnp.zeros_like(token)
    rows = a0.shape[0]
    total = rows
    for i, block in enumerate((a0,)):
        spot = pl.ds(i * rows, rows)
        left[spot], left[pl.ds(total + i * rows, rows)] = halves(block[...])
    z, flip = place[0], place[1]
    for step in range(steps):
        if step + slots - 1 < steps:
            copy(step + slots - 1).start()
        copy(step).wait()
        spot = pl.ds(step * count, count)
        high[:, spot], low[:, spot] = halves(held[step % slots])
        both = dot(left[:, spot], high[:, spot])
        sums = both[:total] + both[total:] + dot(left[:total, spot], low[:, spot])
        for i, (kind, d) in enumerate(plan):
            at = (kind ^ flip, lax.rem(z + d + NZ, NZ))
            part = sums[i * rows : (i + 1) * rows]
            out[at] = part if step == 0 else out[at] + part


def first_group(plan, place, blocks, integrals):
    rows, width = blocks[0].shape
    columns = integrals.shape[0]
    return pl.pallas_call(
        functools.partial(first_kernel, plan),
        out_shape=[
            jax.ShapeDtypeStruct((2, NZ, rows, columns), jnp.float32),
            jax.ShapeDtypeStruct((8, 128), jnp.float32),
            jax.ShapeDtypeStruct(integrals.shape, jnp.bfloat16),
            jax.ShapeDtypeStruct(integrals.shape, jnp.bfloat16),
        ],
        in_specs=[SMEM, VMEM, HBM],
        out_specs=[VMEM] * 4,
        scratch_shapes=[
            pltpu.VMEM((2 * rows, width), jnp.bfloat16),
            pltpu.VMEM((4, columns, width // 8), jnp.float32),
            pltpu.SemaphoreType.DMA((4,)),
        ],
        compiler_params=pltpu.CompilerParams(vmem_limit_bytes=34 * MIB),
        cost_estimate=pl.CostEstimate(flops=48 * rows * columns * width, bytes_accessed=12 * MIB, transcendentals=0),
    )(place, *blocks, integrals)


def stage_kernel(kept, cuts, *refs):
    inputs, outputs = refs[: len(refs) - kept - len(cuts)], refs[len(refs) - len(cuts) :]
    for out, parts in zip(outputs, cuts):
        at = 0
        for source, first, count, *span in parts:
            out[at : at + count] = inputs[source][first : first + count, slice(*(span or (None,)))]
            at += count


def stage(kept, others, cuts, weights, tokens):
    width = kept[0].shape[1]

    def shape(parts):
        span = parts[0][3:] or (0, width)
        return jax.ShapeDtypeStruct((sum(p[2] for p in parts), span[1] - span[0]), jnp.float32)

    return pl.pallas_call(
        functools.partial(stage_kernel, len(kept), cuts),
        out_shape=[jax.ShapeDtypeStruct(v.shape, v.dtype) for v in kept]
        + [shape(parts) for parts in cuts],
        in_specs=[VMEM] * (len(kept) + len(others) + len(weights)) + [ANY] * len(tokens),
        out_specs=[VMEM] * (len(kept) + len(cuts)),
        input_output_aliases={i: i for i in range(len(kept))},
        compiler_params=pltpu.CompilerParams(vmem_limit_bytes=4 * MIB),
        cost_estimate=pl.CostEstimate(flops=0, bytes_accessed=MIB, transcendentals=0),
    )(*kept, *others, *weights, *tokens)


def local(amplitudes, integrals, pair_energy, virt_energy):
    rows, width = amplitudes.shape
    columns = integrals.shape[0]
    half = rows // 2
    quarter = half // 2
    row, col, depth = (lax.axis_index(name) for name in ("row", "col", "depth"))
    z, h = row // NXH, row % NXH
    y, x = col // NXL, col % NXL
    place = jnp.stack([z, h ^ depth]).astype(jnp.int32)

    def ring(up, down):
        return z_shift(up, -1), z_shift(down, 1)

    def whole(kind, d, name):
        return (kind, d, ((name, 0, rows),), 0)

    def early(d, name):
        return (1, d, ((name, 0, half),), 0)

    def lates(d, name):
        return [(1, d, ((name, 0, half),), half), (1, -d, ((name, half, half),), half)]

    late = ((0, half, half), (1, half, half))
    a1 = ring(amplitudes, amplitudes)
    x0 = x_peer(amplitudes)
    partial, token, *weights = first_group(((0, 0),), place, [amplitudes], integrals)
    *a1, b0, late1 = stage(a1, [x0], (((2, 0, half),), late), weights, [token])
    a2 = ring(*a1)
    x1 = x_peer(late1)
    partial, token = group(
        [whole(0, 1, "u"), whole(0, -1, "d"), whole(1, 0, "x0")],
        place, dict(u=a1[0], d=a1[1], x0=x0), weights, partial, rows)
    (b0,) = stage([b0], [], (), weights, [token])
    b1 = ring(b0, b0)
    *a2, late2 = stage(a2, [], (late,), weights, [x1])
    a3 = ring(*a2)
    x2 = x_peer(late2)
    partial, token = group(
        [whole(0, 2, "u"), whole(0, -2, "d"), *lates(1, "x"), early(1, "bu"), early(-1, "bd")],
        place, dict(u=a2[0], d=a2[1], x=x1, bu=b1[0], bd=b1[1]), weights, partial, rows)
    b1 = stage(b1, [], (), weights, [token])
    b2 = ring(*b1)
    *a3, up, down, late3 = stage(a3, [], (((0, 0, rows, 0, width // 2),), ((1, 0, rows, width // 2, width),), late), weights, [x2])
    a4 = z_shift(up, -1), z_shift(down, 1)
    x3 = x_peer(late3)
    b2 = stage(b2, [], (), weights, [late3])
    b3 = ring(*b2)
    x4 = x_peer(a4[0]), x_peer(a4[1])
    partial, token = group(
        [
            whole(0, 3, "a3u"), whole(0, -3, "a3d"), *lates(2, "x2"), early(2, "b2u"), early(-2, "b2d"),
            (0, 4, (("a4u a4d", 0, rows),), 0), early(3, "b3u"), early(-3, "b3d"), *lates(3, "x3"),
        ],
        place,
        dict(a3u=a3[0], a3d=a3[1], x2=x2, b2u=b2[0], b2d=b2[1], a4u=a4[0], a4d=a4[1], b3u=b3[0], b3d=b3[1], x3=x3),
        weights, partial, rows)
    partial, token = group([whole(1, 4, "y")], place, dict(y=x4[0]), weights, partial, rows)
    partial, token = group([whole(1, 4, "y")], place, dict(y=x4[1]), weights, partial, rows, width // 2, True)

    total = (partial[0] + core_peer(partial[1])).reshape(NY, NXL, rows, columns)

    def part(dy, dx):
        at = ((y + dy) % NY, x ^ dx, 0, 0)
        return lax.dynamic_slice(total, at, (1, 1, rows, columns)).reshape(rows, columns)

    others = [(2, 1), (2, 0), (1, 1), (-1, 1), (1, 0), (-1, 0), (0, 1)]
    total = sum((col_shift(part(*step), *step) for step in others), start=part(0, 0))
    return total / (pair_energy[:, None] - virt_energy[None, :])


def solution(mesh):
    in_specs = (
        P("row", ("col", "depth")),
        P("row", ("col", "depth")),
        P(("col", "depth")),
        P("row"),
    )
    out_specs = P(("col", "depth"), "row")
    return jax.shard_map(local, mesh=mesh, in_specs=in_specs, out_specs=out_specs, check_vma=False)
```

```python
import functools

import jax
import jax.numpy as jnp
from jax import lax
from jax.experimental import pallas as pl
from jax.experimental.pallas import tpu as pltpu
from jax.sharding import PartitionSpec as P

NZ, NXH, NY, NXL = 8, 2, 4, 2
MIB = 1 << 20
VMEM = pl.BlockSpec(memory_space=pltpu.VMEM)
SMEM = pl.BlockSpec(memory_space=pltpu.SMEM)
HBM = pl.BlockSpec(memory_space=pltpu.HBM)
ANY = pl.BlockSpec(memory_space=pl.ANY)


def z_shift(block, step):
    perm = [(z * NXH + h, ((z + step) % NZ) * NXH + h) for z in range(NZ) for h in range(NXH)]
    return lax.ppermute(block, "row", perm)


def x_peer(block):
    perm = [(z * NXH + h, z * NXH + 1 - h) for z in range(NZ) for h in range(NXH)]
    return lax.ppermute(block, "row", perm)


def col_shift(block, dy, dx):
    perm = [(y * NXL + x, ((y + dy) % NY) * NXL + (x ^ dx)) for y in range(NY) for x in range(NXL)]
    return lax.ppermute(block, "col", perm)


def core_peer(block):
    return lax.ppermute(block, "depth", [(0, 1), (1, 0)])


def halves(values):
    high = values.astype(jnp.bfloat16)
    return high, (values - high.astype(jnp.float32)).astype(jnp.bfloat16)


def dot(a, b):
    return lax.dot_general(a, b, (((1,), (1,)), ((), ())), preferred_element_type=jnp.float32)


def names_of(plan):
    return sorted({name for _, _, pieces, _ in plan for both, *_ in pieces for name in both.split()})


def group_kernel(plan, place, *refs, held, first, adding):
    names = names_of(plan)
    blocks = dict(zip(names, refs))
    high, low = refs[len(names) : len(names) + 2]
    out, token, left = refs[-3:]
    span = pl.ds(first, left.shape[1])
    token[...] = jnp.zeros_like(token)
    total = left.shape[0] // 2
    at = 0
    for kind, d, pieces, start in plan:
        values = [
            jnp.concatenate([blocks[name][low_row : low_row + count] for name in both.split()], axis=1)
            for both, low_row, count in pieces
        ]
        values = values[0] if len(values) == 1 else jnp.concatenate(values)
        count = values.shape[0]
        left[at : at + count], left[total + at : total + at + count] = halves(values)
        at += count
    z, flip = place[0], place[1]

    def tile(n, _):
        spot = pl.ds(pl.multiple_of(n * 768, 768), 768)
        both = dot(left[...], high[spot, span])
        sums = both[:total] + both[total:] + dot(left[:total], low[spot, span])
        at = 0
        for kind, d, pieces, start in plan:
            count = sum(p[2] for p in pieces)
            where = (kind ^ flip, lax.rem(z + d + NZ, NZ), slice(start, start + count), spot)
            out[where] = sums[at : at + count] + out[where] if adding else sums[at : at + count]
            at += count
        return 0

    lax.fori_loop(0, high.shape[0] // 768, tile, 0)


def group(plan, place, blocks, weights, partial, rows, first=0, adding=False, lead=(2, NZ)):
    names = names_of(plan)
    columns = weights[0].shape[0]
    width = max(block.shape[1] for block in blocks.values())
    total = sum(p[2] for _, _, pieces, _ in plan for p in pieces)
    operands = [place] + [blocks[name] for name in names] + list(weights)
    in_specs = [SMEM] + [VMEM] * (len(names) + 2)
    aliases = {}
    if partial is not None:
        aliases = {len(operands): 0}
        operands.append(partial)
        in_specs.append(VMEM)
    return pl.pallas_call(
        functools.partial(group_kernel, plan, held=partial is not None, first=first, adding=adding),
        out_shape=[
            jax.ShapeDtypeStruct((*lead, rows, columns), jnp.float32),
            jax.ShapeDtypeStruct((8, 128), jnp.float32),
        ],
        in_specs=in_specs,
        out_specs=[VMEM, VMEM],
        scratch_shapes=[pltpu.VMEM((2 * total, width), jnp.bfloat16)],
        input_output_aliases=aliases,
        compiler_params=pltpu.CompilerParams(vmem_limit_bytes=10 * MIB),
        cost_estimate=pl.CostEstimate(flops=4 * 3 * total * columns * width, bytes_accessed=MIB, transcendentals=0),
    )(*operands)


def first_kernel(plan, place, a0, source, out, token, high, low, left, held, sems):
    steps, slots = 8, held.shape[0]
    count = source.shape[1] // steps

    def copy(step):
        slot = step % slots
        return pltpu.make_async_copy(source.at[:, pl.ds(step * count, count)], held.at[slot], sems.at[slot])

    for step in range(slots - 1):
        copy(step).start()
    token[...] = jnp.zeros_like(token)
    rows = a0.shape[0]
    total = rows
    for i, block in enumerate((a0,)):
        spot = pl.ds(i * rows, rows)
        left[spot], left[pl.ds(total + i * rows, rows)] = halves(block[...])
    z, flip = place[0], place[1]
    out[1 ^ flip, lax.rem(z + NZ // 2, NZ)] = jnp.zeros(out.shape[2:], jnp.float32)
    for step in range(steps):
        if step + slots - 1 < steps:
            copy(step + slots - 1).start()
        copy(step).wait()
        spot = pl.ds(step * count, count)
        high[:, spot], low[:, spot] = halves(held[step % slots])
        both = dot(left[:, spot], high[:, spot])
        sums = both[:total] + both[total:] + dot(left[:total, spot], low[:, spot])
        for i, (kind, d) in enumerate(plan):
            at = (kind ^ flip, lax.rem(z + d + NZ, NZ))
            part = sums[i * rows : (i + 1) * rows]
            out[at] = part if step == 0 else out[at] + part


def first_group(plan, place, blocks, integrals):
    rows, width = blocks[0].shape
    columns = integrals.shape[0]
    return pl.pallas_call(
        functools.partial(first_kernel, plan),
        out_shape=[
            jax.ShapeDtypeStruct((2, NZ, rows, columns), jnp.float32),
            jax.ShapeDtypeStruct((8, 128), jnp.float32),
            jax.ShapeDtypeStruct(integrals.shape, jnp.bfloat16),
            jax.ShapeDtypeStruct(integrals.shape, jnp.bfloat16),
        ],
        in_specs=[SMEM, VMEM, HBM],
        out_specs=[VMEM] * 4,
        scratch_shapes=[
            pltpu.VMEM((2 * rows, width), jnp.bfloat16),
            pltpu.VMEM((4, columns, width // 8), jnp.float32),
            pltpu.SemaphoreType.DMA((4,)),
        ],
        compiler_params=pltpu.CompilerParams(vmem_limit_bytes=34 * MIB),
        cost_estimate=pl.CostEstimate(flops=48 * rows * columns * width, bytes_accessed=12 * MIB, transcendentals=0),
    )(place, *blocks, integrals)


def stage_kernel(kept, cuts, *refs):
    inputs, outputs = refs[: len(refs) - kept - len(cuts)], refs[len(refs) - len(cuts) :]
    for out, parts in zip(outputs, cuts):
        at = 0
        for source, first, count, *span in parts:
            out[at : at + count] = inputs[source][first : first + count, slice(*(span or (None,)))]
            at += count


def stage(kept, others, cuts, weights, tokens):
    width = kept[0].shape[1]

    def shape(parts):
        span = parts[0][3:] or (0, width)
        return jax.ShapeDtypeStruct((sum(p[2] for p in parts), span[1] - span[0]), jnp.float32)

    return pl.pallas_call(
        functools.partial(stage_kernel, len(kept), cuts),
        out_shape=[jax.ShapeDtypeStruct(v.shape, v.dtype) for v in kept]
        + [shape(parts) for parts in cuts],
        in_specs=[VMEM] * (len(kept) + len(others) + len(weights)) + [ANY] * len(tokens),
        out_specs=[VMEM] * (len(kept) + len(cuts)),
        input_output_aliases={i: i for i in range(len(kept))},
        compiler_params=pltpu.CompilerParams(vmem_limit_bytes=4 * MIB),
        cost_estimate=pl.CostEstimate(flops=0, bytes_accessed=MIB, transcendentals=0),
    )(*kept, *others, *weights, *tokens)


def local(amplitudes, integrals, pair_energy, virt_energy):
    rows, width = amplitudes.shape
    columns = integrals.shape[0]
    half = rows // 2
    quarter = half // 2
    row, col, depth = (lax.axis_index(name) for name in ("row", "col", "depth"))
    z, h = row // NXH, row % NXH
    y, x = col // NXL, col % NXL
    place = jnp.stack([z, h ^ depth]).astype(jnp.int32)

    def ring(up, down):
        return z_shift(up, -1), z_shift(down, 1)

    def whole(kind, d, name):
        return (kind, d, ((name, 0, rows),), 0)

    def early(d, name):
        return (1, d, ((name, 0, half),), 0)

    def lates(d, name):
        return [(1, d, ((name, 0, half),), half), (1, -d, ((name, half, half),), half)]

    late = ((0, half, half), (1, half, half))
    a1 = ring(amplitudes, amplitudes)
    x0 = x_peer(amplitudes)
    partial, token, *weights = first_group(((0, 0),), place, [amplitudes], integrals)
    *a1, b0, late1 = stage(a1, [x0], (((2, 0, half),), late), weights, [token])
    a2 = ring(*a1)
    x1 = x_peer(late1)
    partial, token = group(
        [whole(0, 1, "u"), whole(0, -1, "d"), whole(1, 0, "x0")],
        place, dict(u=a1[0], d=a1[1], x0=x0), weights, partial, rows)
    (b0,) = stage([b0], [], (), weights, [token])
    b1 = ring(b0, b0)
    *a2, late2 = stage(a2, [], (late,), weights, [x1])
    a3 = ring(*a2)
    x2 = x_peer(late2)
    partial, token = group(
        [whole(0, 2, "u"), whole(0, -2, "d"), *lates(1, "x"), early(1, "bu"), early(-1, "bd")],
        place, dict(u=a2[0], d=a2[1], x=x1, bu=b1[0], bd=b1[1]), weights, partial, rows)
    b1 = stage(b1, [], (), weights, [token])
    b2 = ring(*b1)
    *a3, up, down, late3 = stage(a3, [], (((0, 0, rows, 0, width // 2),), ((1, 0, rows, width // 2, width),), late), weights, [x2])
    a4 = z_shift(up, -1), z_shift(down, 1)
    x3 = x_peer(late3)
    b2 = stage(b2, [], (), weights, [late3])
    b3 = ring(*b2)
    x4 = x_peer(a4[0]), x_peer(a4[1])
    partial, token = group(
        [
            whole(0, 3, "a3u"), whole(0, -3, "a3d"), *lates(2, "x2"), early(2, "b2u"), early(-2, "b2d"),
            (0, 4, (("a4u a4d", 0, rows),), 0), early(3, "b3u"), early(-3, "b3d"), *lates(3, "x3"),
        ],
        place,
        dict(a3u=a3[0], a3d=a3[1], x2=x2, b2u=b2[0], b2d=b2[1], a4u=a4[0], a4d=a4[1], b3u=b3[0], b3d=b3[1], x3=x3),
        weights, partial, rows)
    total = partial[0] + core_peer(partial[1])
    origin = jnp.zeros_like(place)
    last, token = group([whole(0, 0, "y")], origin, dict(y=x4[0]), weights, None, rows, lead=(1, 1))
    last, token = group([whole(0, 0, "y")], origin, dict(y=x4[1]), weights, last, rows, width // 2, True, (1, 1))
    last = last[0, 0]
    last = jnp.where(h ^ depth == 1, last + core_peer(last), 0.0)
    far = (z + NZ // 2) % NZ == jnp.arange(NZ)
    total = (total + jnp.where(far[:, None, None], last[None], 0.0)).reshape(NY, NXL, rows, columns)

    def part(dy, dx):
        at = ((y + dy) % NY, x ^ dx, 0, 0)
        return lax.dynamic_slice(total, at, (1, 1, rows, columns)).reshape(rows, columns)

    others = [(2, 1), (2, 0), (1, 1), (-1, 1), (1, 0), (-1, 0), (0, 1)]
    total = sum((col_shift(part(*step), *step) for step in others), start=part(0, 0))
    return total / (pair_energy[:, None] - virt_energy[None, :])


def solution(mesh):
    in_specs = (
        P("row", ("col", "depth")),
        P("row", ("col", "depth")),
        P(("col", "depth")),
        P("row"),
    )
    out_specs = P(("col", "depth"), "row")
    return jax.shard_map(local, mesh=mesh, in_specs=in_specs, out_specs=out_specs, check_vma=False)
```
